128 devices in a mesh: expert: 32 (over x, z, core), tensor: 4 (over y).
Axes of the slice: x: 4, y: 4, z: 4, core: 2. Of those that a mesh axis runs over, the one named last changes fastest.
Arguments:
- tokens: bfloat16 [16384, 2048], P('expert'), may hold values from -40 to 40
- norm_gain: float32 [2048], replicated, may hold values from 0.5 to 1.5
- expert_ids: int32 [16384, 8], P('expert'), may hold values from 0 to 127, all different within a row; in each aligned block of 512 rows (0 to 511, 512 to 1023, ...) at most 34 rows name the same one
- route_weights: float32 [16384, 8], P('expert'), may hold values from 0.5 to 1
- w_gate: bfloat16 [128, 2048, 768], P('expert', None, 'tensor'), may hold values from -0.125 to 0.125
- w_up: bfloat16 [128, 2048, 768], P('expert', None, 'tensor'), may hold values from -0.125 to 0.125
- w_down: bfloat16 [128, 768, 2048], P('expert', 'tensor'), may hold values from -0.21875 to 0.21875
- codec_embeds: bfloat16 [32768, 1024], P(('expert', 'tensor')), may hold values from -30 to 30
- frame_lengths: int32 [64], P('expert'), may hold values from 128 to 896, as said below
- source_rows: int32 [32768], P(('expert', 'tensor')), may hold values from 0 to 16383, as said below
- w_handover: bfloat16 [2048, 1024], replicated, may hold values from -0.125 to 0.125
- talker_gain: float32 [1024], replicated, may hold values from 0.5 to 1.5
- w_query: bfloat16 [1024, 1024], replicated, may hold values from -1 to 1
- w_kv: bfloat16 [1024, 1024], replicated, may hold values from -1 to 1
- qk_gains: float32 [2, 128], replicated, may hold values from 1 to 5
- w_out: bfloat16 [1024, 1024], replicated, may hold values from -0.1875 to 0.1875
Outputs:
- thinker_out: bfloat16 [16384, 2048], P(('expert', 'tensor'))
- talker_out: bfloat16 [32768, 1024], P(('expert', 'tensor'))
The draws below stay inside these ranges and needn't reach their ends.
Inputs may be any that keep to these rules, and one draw needn't show every extreme that they name: `expert_ids`: in each aligned block of 512 tokens no expert is named by more than 34 routes, and in every draw some expert is named by exactly 34 routes of some block. `frame_lengths`: entries 2 g and 2 g + 1 are the frame counts of the two dialogues of group g and sum to 1024. `source_rows`: A frame of group g reads one of the thinker rows g * 512 to (g + 1) * 512 - 1; along the frames of one dialogue the rows never fall.
All inputs are finite; a program needn't handle non-finite values.
Results may differ from the reference program's by a relative error of at most 0.04.
Values may be sent and summed in bfloat16 or wider, within the bound.
A program may use at most 192 MiB of HBM per device.

```python
import math
import jax
import jax.numpy as jnp
import numpy as np
from jax import lax

D = 2048
FF = 768
EXPERTS = 128
TOPK = 8
TOK_DEV = 512
TOKENS = 16384
CAP = 34
FF_PART = 192
TW = 1024
HEADS = 8
KV_HEADS = 4
HEAD = 128
GROUP_FRAMES = 1024
FRAMES = 32768
DIALOGS = 64
N_EXPERT = 32
N_TENSOR = 4


def scaled_rows(key, row_count, col_count, row_lo, row_hi, limit):
    first_key, second_key, third_key = jax.random.split(key, 3)
    base = jax.random.normal(first_key, (row_count, col_count), jnp.float32)
    row_scale = jnp.exp(jax.random.uniform(second_key, (row_count, 1), jnp.float32, math.log(row_lo), math.log(row_hi)))
    col_scale = jnp.exp(jax.random.uniform(third_key, (1, col_count), jnp.float32, math.log(0.5), math.log(2.0)))
    return jnp.clip(base * row_scale * col_scale, -limit, limit)


def draw_tokens(key, part):
    return scaled_rows(jax.random.fold_in(key, 11), TOKENS, D, 0.5, 5.0, 40.0).astype(jnp.bfloat16)


def draw_codec_embeds(key, part):
    return scaled_rows(jax.random.fold_in(key, 13), FRAMES, TW, 0.3, 3.0, 30.0).astype(jnp.bfloat16)


def talker_weights(key):
    base = jax.random.fold_in(key, 31)
    first_key, second_key, third_key = jax.random.split(base, 3)
    scale = TW ** (-0.5)
    queries = jax.random.normal(first_key, (TW, HEADS * HEAD), jnp.float32) * scale
    key_part = jax.random.normal(second_key, (TW, KV_HEADS * HEAD), jnp.float32) * scale
    value_part = jax.random.normal(third_key, (TW, KV_HEADS * HEAD), jnp.float32) * scale
    return (jnp.clip(queries, -1.0, 1.0), jnp.clip(jnp.concatenate([key_part, value_part], axis=1), -1.0, 1.0))


def draw_w_query(key, part):
    return talker_weights(key)[0].astype(jnp.bfloat16)


def draw_w_kv(key, part):
    return talker_weights(key)[1].astype(jnp.bfloat16)


def draw_qk_gains(key, part):
    gain_key = jax.random.fold_in(key, 43)
    return jax.random.uniform(gain_key, (2, HEAD), jnp.float32, 1.0, 1.5)


def frame_plan(key):
    base = jax.random.fold_in(key, 57)
    first_key, second_key, third_key = jax.random.split(base, 3)
    group_count = DIALOGS // 2
    margin = GROUP_FRAMES // 8
    spread = GROUP_FRAMES - 2 * margin
    offset = jax.random.randint(first_key, (group_count,), 0, spread + 1, jnp.int32)
    order = jax.random.permutation(second_key, group_count)
    offset = offset.at[order[0]].set(spread).at[order[1]].set(0)
    first_length = margin + offset
    split_rows = jax.random.randint(third_key, (group_count,), TOK_DEV // 4, 3 * TOK_DEV // 4 + 1, jnp.int32)
    lengths = jnp.stack([first_length, GROUP_FRAMES - first_length], axis=1).reshape(group_count * 2)
    positions = jnp.arange(GROUP_FRAMES, dtype=jnp.int32)[None, :]
    later = positions >= first_length[:, None]
    inner = positions - jnp.where(later, first_length[:, None], 0)
    frame_total = jnp.where(later, GROUP_FRAMES - first_length[:, None], first_length[:, None])
    row_start = jnp.where(later, split_rows[:, None], 0)
    row_span = jnp.where(later, TOK_DEV - split_rows[:, None], split_rows[:, None])
    group_base = jnp.arange(group_count, dtype=jnp.int32)[:, None] * TOK_DEV
    row_index = group_base + row_start + inner * row_span // frame_total
    return (lengths.astype(jnp.int32), row_index.reshape(group_count * GROUP_FRAMES).astype(jnp.int32))


def draw_frame_lengths(key, part):
    return frame_plan(key)[0]


def draw_source_rows(key, part):
    return frame_plan(key)[1]


def block_levels(stream_key, extent, cuts, smallest, largest):
    factor_of = 1.0
    for position, blocks in cuts:
        heights = jax.random.uniform(jax.random.fold_in(jax.random.fold_in(stream_key, 6), position), (blocks,), jnp.float32, smallest / len(cuts), largest / len(cuts))
        factor_of = factor_of * jnp.repeat(jnp.exp(heights), extent[position] // blocks).reshape((-1,) + (1,) * (len(extent) - 1 - position))
    return factor_of


def deal_out(own_key, own, number, rows, count, top, most, lean):
    ranking = jax.random.permutation(own_key, count)
    crowded, ordinary = shares(count, rows * top, most, lean, True), shares(count, rows * top, most, lean, False)
    places = jnp.arange(count)

    def named(sizes, rotation):
        used = int((sizes > 0).sum())
        fixed = max(1, used // 4)
        shifted = fixed + (places - fixed + rotation * (used - fixed)) % max(1, count - fixed)
        return jnp.zeros((count,), jnp.int32).at[ranking[jnp.where(places < fixed, places, shifted)]].set(jnp.asarray(sizes, jnp.int32))

    sizes = jnp.where(number % 4 == 0, named(crowded, number // 4), named(ordinary, number - number // 4 - 1))
    mixed = jax.random.permutation(jax.random.fold_in(own, 3), count)
    source_of, receiver = mixed[0:count // 2 * 2:2], mixed[1:count // 2 * 2:2]
    room = jnp.minimum(sizes[source_of] - 1, most - sizes[receiver]) // 2
    room = jnp.where((source_of == ranking[0]) | (receiver == ranking[0]) | (sizes[receiver] == 0), 0, jnp.maximum(room, 0))
    shifted = jax.random.randint(jax.random.fold_in(own, 4), (count // 2,), 0, 1 << 20) % (room + 1)
    sizes = sizes.at[source_of].add(-shifted).at[receiver].add(shifted)
    members = jnp.searchsorted(jnp.cumsum(sizes), jnp.arange(rows * top), side="right").astype(jnp.int32)
    listing = members.reshape(top, rows).T
    listing = listing[jax.random.permutation(jax.random.fold_in(own, 1), rows)]
    rotation = jax.random.randint(jax.random.fold_in(own, 2), (rows, 1), 0, top)
    return jnp.take_along_axis(listing, (jnp.arange(top)[None, :] + rotation) % top, axis=1)


def shares(amount, total, most, lean, full):
    loads = [(1 << 20) // math.isqrt(standing ** lean) + 1 for standing in range(1, amount + 1)]
    largest = most if full else min(most, max(-(-total // amount), total * loads[0] // sum(loads)))
    least = 1 if total - largest >= amount - 1 else 0
    given, spare = [largest] + [least] * (amount - 1), total - largest - least * (amount - 1)
    while spare > 0:
        candidates = [i for i in range(1, amount) if given[i] < largest] or [i for i in range(1, amount) if given[i] < most]
        whole, remaining = sum([loads[i] for i in candidates]), spare
        for i in candidates:
            more = min(most - given[i], max(1, remaining * loads[i] // whole), spare)
            given[i] = given[i] + more
            spare = spare - more
    return np.array(given)


def normal_values(stream_key, shape, scale, reach, shards=(), kind=jnp.bfloat16):
    entries = scale * jax.random.normal(stream_key, shape, jnp.float32)
    if shards:
        entries = entries * block_levels(stream_key, shape, shards, -0.22, 0.18)
    return jnp.clip(entries, -reach, reach).astype(kind)


def setup_inputs(seed: int = 0) -> dict:
    seeds = jax.random.split(jax.random.key(seed), 17)
    tokens = draw_tokens(jax.random.fold_in(seeds[16], 71), 0)
    norm_gain = jnp.clip(1.0 + 0.1 * jax.random.normal(seeds[1], (D,), jnp.float32), 0.5, 1.5)
    expert_ids_keys = jax.random.split(jax.random.fold_in(seeds[2], 1), TOKENS // TOK_DEV)
    expert_ids_turns = jax.random.permutation(jax.random.fold_in(seeds[2], 3), TOKENS // TOK_DEV)
    expert_ids = jax.vmap(lambda own, number: deal_out(jax.random.fold_in(seeds[2], 2), own, number, TOK_DEV, EXPERTS, TOPK, CAP, 1))(expert_ids_keys, expert_ids_turns).reshape((TOKENS, TOPK))
    route_weights = jnp.clip(0.5 + 0.5 * jax.random.uniform(seeds[3], (TOKENS, TOPK), jnp.float32) ** block_levels(seeds[3], (TOKENS, TOPK), ((0, 32),), -0.2, 0.2), 0.5, 1.0)
    w_gate = normal_values(seeds[4], (EXPERTS, D, FF), D ** -0.5, 0.125, ((0, 32), (2, 4)))
    w_up = normal_values(seeds[5], (EXPERTS, D, FF), D ** -0.5, 0.125, ((0, 32), (2, 4)))
    w_down = normal_values(seeds[6], (EXPERTS, FF, D), FF ** -0.5, 0.21875, ((0, 32), (1, 4)))
    codec_embeds = draw_codec_embeds(jax.random.fold_in(seeds[16], 71), 0)
    frame_lengths = draw_frame_lengths(jax.random.fold_in(seeds[16], 71), 0)
    source_rows = draw_source_rows(jax.random.fold_in(seeds[16], 71), 0)
    w_handover = normal_values(seeds[10], (D, TW), D ** -0.5, 0.125)
    talker_gain = jnp.clip(1.0 + 0.1 * jax.random.normal(seeds[11], (TW,), jnp.float32), 0.5, 1.5)
    w_query = draw_w_query(jax.random.fold_in(seeds[16], 71), 0)
    w_kv = draw_w_kv(jax.random.fold_in(seeds[16], 71), 0)
    qk_gains = draw_qk_gains(jax.random.fold_in(seeds[16], 71), 0)
    w_out = normal_values(seeds[15], (HEADS * HEAD, TW), (HEADS * HEAD) ** -0.5, 0.1875)
    return dict(tokens=tokens, norm_gain=norm_gain, expert_ids=expert_ids, route_weights=route_weights, w_gate=w_gate, w_up=w_up, w_down=w_down, codec_embeds=codec_embeds, frame_lengths=frame_lengths, source_rows=source_rows, w_handover=w_handover, talker_gain=talker_gain, w_query=w_query, w_kv=w_kv, qk_gains=qk_gains, w_out=w_out)


epsilon = 1e-06

def rms_scale(values, gain):
    mean_square = lax.optimization_barrier(jnp.mean(values * values, axis=-1, keepdims=True))
    return values * lax.rsqrt(mean_square + epsilon) * gain

def reference(tokens, norm_gain, expert_ids, route_weights, w_gate, w_up, w_down, codec_embeds, frame_lengths, source_rows, w_handover, talker_gain, w_query, w_kv, qk_gains, w_out):
    normed = rms_scale(tokens.astype(jnp.float32), norm_gain).astype(jnp.bfloat16)
    padded = jnp.concatenate([normed, jnp.zeros((1, D), jnp.bfloat16)], axis=0)
    route_count = TOK_DEV * TOPK
    grouped_ids = expert_ids.reshape(N_EXPERT, route_count)
    one_hot = (grouped_ids[:, :, None] == jnp.arange(EXPERTS, dtype=jnp.int32)[None, None, :]).astype(jnp.int32)
    before = jnp.cumsum(one_hot, axis=1) - one_hot
    slot_rank = lax.optimization_barrier(jnp.sum(before * one_hot, axis=2)).astype(jnp.int32)
    group_ids = jnp.arange(N_EXPERT, dtype=jnp.int32)[:, None]
    anchor = group_ids * TOK_DEV + jnp.arange(route_count, dtype=jnp.int32)[None, :] // TOPK
    column = grouped_ids * (N_EXPERT * CAP) + group_ids * CAP + slot_rank
    route_share = route_weights / lax.optimization_barrier(jnp.sum(route_weights, axis=1, keepdims=True))
    token_table = jnp.full((EXPERTS * N_EXPERT * CAP,), TOKENS, jnp.int32)
    token_table = token_table.at[column.reshape(-1)].set(anchor.reshape(-1))
    weight_table = jnp.zeros((EXPERTS * N_EXPERT * CAP,), jnp.float32)
    weight_table = weight_table.at[column.reshape(-1)].set(route_share.reshape(-1))
    token_table = token_table.reshape(EXPERTS, N_EXPERT * CAP)
    weight_table = weight_table.reshape(EXPERTS, N_EXPERT * CAP)

    def one_expert(mixed, inputs):
        gate_weight, up_weight, down_weight, indices, scales = inputs
        block_rows = padded[indices]
        gate_proj = jnp.dot(block_rows, gate_weight, preferred_element_type=jnp.float32)
        up_proj = jnp.dot(block_rows, up_weight, preferred_element_type=jnp.float32)
        hidden = (jax.nn.silu(gate_proj) * up_proj).astype(jnp.bfloat16)
        pieces = jnp.einsum('rsf,sfd->srd', hidden.reshape(N_EXPERT * CAP, N_TENSOR, FF_PART).astype(jnp.float32), down_weight.reshape(N_TENSOR, FF_PART, D).astype(jnp.float32))
        rounded = lax.optimization_barrier(pieces.astype(jnp.bfloat16)).astype(jnp.float32)
        expert_sum = lax.optimization_barrier(jnp.sum(rounded, axis=0))
        mixed = mixed.at[indices].add(scales[:, None] * expert_sum, mode='drop')
        return (mixed, None)
    mixed = lax.scan(one_expert, jnp.zeros((TOKENS, D), jnp.float32), (w_gate, w_up, w_down, token_table, weight_table))[0]
    thinker_out = mixed.astype(jnp.bfloat16)
    handed = jnp.dot(thinker_out[source_rows], w_handover, preferred_element_type=jnp.float32).astype(jnp.bfloat16)
    talker_in = handed.astype(jnp.float32) + codec_embeds.astype(jnp.float32)
    talker_normed = rms_scale(talker_in, talker_gain).astype(jnp.bfloat16)
    queries = jnp.dot(talker_normed, w_query, preferred_element_type=jnp.float32)
    key_value = jnp.dot(talker_normed, w_kv, preferred_element_type=jnp.float32)
    group_size = HEADS // KV_HEADS
    query_heads = rms_scale(queries.reshape(N_EXPERT, GROUP_FRAMES, KV_HEADS, group_size, HEAD), qk_gains[0]).astype(jnp.bfloat16)
    key_heads = rms_scale(key_value[:, :KV_HEADS * HEAD].reshape(N_EXPERT, GROUP_FRAMES, KV_HEADS, HEAD), qk_gains[1]).astype(jnp.bfloat16)
    value_heads = key_value[:, KV_HEADS * HEAD:].astype(jnp.bfloat16).reshape(N_EXPERT, GROUP_FRAMES, KV_HEADS, HEAD)
    positions = jnp.arange(GROUP_FRAMES, dtype=jnp.int32)
    first_length = frame_lengths.reshape(N_EXPERT, 2)[:, 0]

    def one_group(inputs):
        query_block, key_block, value_block, split = inputs
        scores = jnp.einsum('fgrh,kgh->grfk', query_block.astype(jnp.float32), key_block.astype(jnp.float32)) * HEAD ** (-0.5)
        later = positions >= split
        allowed = (later[:, None] == later[None, :]) & (positions[None, :] <= positions[:, None])
        masked = jnp.where(allowed[None, None], scores, -jnp.inf)
        row_peak = lax.optimization_barrier(jnp.max(masked, axis=-1, keepdims=True))
        exp_weights = jnp.exp(masked - row_peak).astype(jnp.bfloat16)
        denominator = lax.optimization_barrier(jnp.sum(exp_weights.astype(jnp.float32), axis=-1))
        attended = jnp.einsum('grfk,kgh->fgrh', exp_weights.astype(jnp.float32), value_block.astype(jnp.float32))
        return (attended / jnp.transpose(denominator, (2, 0, 1))[..., None]).astype(jnp.bfloat16)
    attended = lax.map(one_group, (query_heads, key_heads, value_heads, first_length)).reshape(FRAMES, HEADS * HEAD)
    talker_out = jnp.dot(attended, w_out, preferred_element_type=jnp.float32).astype(jnp.bfloat16)
    return (thinker_out, talker_out)
```

```python
import functools

import jax
import jax.numpy as jnp
from jax import lax
from jax.experimental import pallas as pl
from jax.experimental.pallas import tpu as pltpu
from jax.sharding import PartitionSpec as P

MESH = pl.DeviceIdType.MESH
BF = jnp.bfloat16
F32 = jnp.float32
EPS = 1e-06
GROUPS = 32
SLOT = 32
CHUNKS = 4
CW = 512


def peer_shifts():
    def opposite(s):
        return ((4 - s[0]) % 4, (4 - s[1]) % 4, s[2])

    every = [
        (dx, dz, dc)
        for dx in range(4)
        for dz in range(4)
        for dc in range(2)
        if (dx, dz, dc) != (0, 0, 0)
    ]
    order, seen = [], set()
    for s in sorted(every, key=lambda s: (sum(min(v, 4 - v) for v in s[:2]), s)):
        for one in (s, opposite(s)):
            if one not in seen:
                seen.add(one)
                order.append(one)
    return order[::-1]


SHIFTS = peer_shifts()
REMOTE = len(SHIFTS)


def mm(a, b):
    return jnp.dot(a, b, preferred_element_type=F32)


def mm_nt(a, b):
    return lax.dot_general(a, b, (((1,), (1,)), ((), ())), preferred_element_type=F32)


def iota(shape, dim):
    return lax.broadcasted_iota(jnp.int32, shape, dim)


def ones_where(cond):
    return jnp.where(cond, 1.0, 0.0).astype(BF)


def rms(v, gain):
    return v * lax.rsqrt(jnp.mean(v * v, axis=-1, keepdims=True) + EPS) * gain


def kernel(
    tok_hbm, gain, ids, rw, wg_hbm, wu_hbm, wd_hbm, codec_hbm, flen, src, wh_hbm, tgain, wq_hbm, wkv_hbm, qkg, wo_hbm,
    thinker, talker,
    tok, wg, wu, wd, wh, wq, wkv, wo, pw, sel, sb, xb, hb, rb, rem_s, rem_r, orem, rrem, ps, pr,
    hacc, ha, codec, srcs, oh, tn, kb, vb, bias, qb, at, acc_o,
    own_sem, wsend, wrecv, dsend, drecv, rsend, rrecv, psend, precv, hsend, hrecv, csend, crecv, ssend, srecv,
):
    e = lax.axis_index("expert")
    t = lax.axis_index("tensor")
    x, z, c = e // 8, (e // 2) % 4, e % 2

    def shifted(s, sign):
        return (
            lax.rem(x + sign * s[0] + 4, 4) * 8
            + lax.rem(z + sign * s[1] + 4, 4) * 2
            + lax.rem(c + s[2], 2)
        )

    to = [shifted(s, 1) for s in SHIFTS]
    back = [shifted(s, -1) for s in SHIFTS]
    side = [t] + [lax.rem(t + d, 4) for d in (1, 2, 3)]

    barrier = pltpu.get_barrier_semaphore()
    for j in to:
        pl.semaphore_signal(barrier, inc=1, device_id=(j, t), device_id_type=MESH)
    for d in (1, 2, 3):
        pl.semaphore_signal(barrier, inc=1, device_id=(e, side[d]), device_id_type=MESH)

    local = [
        pltpu.make_async_copy(tok_hbm, tok, own_sem.at[0]),
        pltpu.make_async_copy(wg_hbm.at[t], wg.at[0], own_sem.at[1]),
        pltpu.make_async_copy(wu_hbm.at[t], wu.at[0], own_sem.at[2]),
        pltpu.make_async_copy(wd_hbm.at[t], wd.at[0], own_sem.at[3]),
        pltpu.make_async_copy(wh_hbm, wh, own_sem.at[4]),
        pltpu.make_async_copy(wkv_hbm, wkv, own_sem.at[5]),
        pltpu.make_async_copy(wq_hbm, wq, own_sem.at[6]),
        pltpu.make_async_copy(wo_hbm, wo, own_sem.at[7]),
        pltpu.make_async_copy(codec_hbm, codec.at[t], own_sem.at[8]),
    ]
    for cp in local:
        cp.start()

    def remote(a, b, s, r, device):
        return pltpu.make_async_remote_copy(
            src_ref=a, dst_ref=b, send_sem=s, recv_sem=r, device_id=device, device_id_type=MESH
        )

    pl.semaphore_wait(barrier, REMOTE + 3)

    gate_up = {}
    for d in (1, 3, 2):
        for a, (h, v) in enumerate(((wg_hbm, wg), (wu_hbm, wu))):
            gate_up[a, d] = remote(h.at[side[d]], v.at[d], wsend.at[a, d], wrecv.at[a, d], (e, side[d]))
            gate_up[a, d].start()
    source_copies = [remote(src, srcs.at[t], ssend.at[d], srecv.at[d], (e, side[d])) for d in (1, 2, 3)]
    for cp in source_copies:
        cp.start()
    srcs[t] = src[...]

    slot_row = iota((GROUPS, 512), 0)
    wanted = jnp.full((GROUPS, 512), 4 * e + t, jnp.int32)
    for i in range(REMOTE):
        wanted = jnp.where(slot_row == i, 4 * to[i] + t, wanted)
    total = jnp.sum(rw[...], axis=0, keepdims=True)
    share = rw[...] / total
    chosen = jnp.zeros((GROUPS, 512), F32)
    weight = jnp.zeros((GROUPS, 512), F32)
    for k in range(8):
        hit = ids[k : k + 1, :] == wanted
        chosen = chosen + jnp.where(hit, 1.0, 0.0)
        weight = weight + jnp.where(hit, share[k : k + 1, :], 0.0)
    upper = ones_where(iota((512, 512), 0) < iota((512, 512), 1))
    rank = mm(chosen.astype(BF), upper)
    rank = jnp.where(chosen > 0.5, rank, -1.0).astype(BF)
    weight = weight.astype(BF)

    local[0].wait()

    def norm_tile(i, carry):
        rows = pl.ds(pl.multiple_of(i * 64, 64), 64)
        tok[rows, :] = rms(tok[rows, :].astype(F32), gain[...]).astype(BF)
        return carry

    lax.fori_loop(0, 8, norm_tile, 0)

    def dispatch_tile(i, carry):
        rows = pl.ds(pl.multiple_of(i * 128, 128), 128)
        spread = ones_where(((iota((128, GROUPS), 0) + i * 128) >> 5) == iota((128, GROUPS), 1))
        place = (iota((128, 512), 0) & 31).astype(F32)
        hit = mm(spread, rank) == place
        pw[rows, :] = jnp.where(hit, mm(spread, weight), 0.0).astype(BF)
        sb[rows, :] = mm(ones_where(hit), tok[...]).astype(BF)
        return carry

    lax.fori_loop(0, 8, dispatch_tile, 0)
    dispatch = []
    for i in range(REMOTE):
        cp = remote(
            sb.at[pl.ds(i * SLOT, SLOT)], xb.at[pl.ds(i * SLOT, SLOT)], dsend.at[0], drecv.at[0], (to[i], t)
        )
        cp.start()

    spread = ones_where((iota((64, GROUPS), 0) >> 1) == iota((64, GROUPS), 1))
    place = (iota((64, 512), 0) & 1).astype(F32) + 32.0
    hit = mm(spread, rank) == place
    pw[1024:1088, :] = jnp.where(hit, mm(spread, weight), 0.0).astype(BF)
    extra = mm(ones_where(hit), tok[...]).astype(BF)
    row, col = iota((512, 64), 0), iota((512, 64), 1)
    same = ((row >> 4) == (col >> 1)) & ((row & 1) == (col & 1))
    packed = jnp.zeros((512, 256), F32)
    for q in range(8):
        packed = packed + mm(ones_where(same & (((row >> 1) & 7) == q)), extra[:, q * 256 : (q + 1) * 256])
    rem_s[...] = packed.astype(BF)
    for i in range(REMOTE):
        cp = remote(rem_s.at[pl.ds(i * 16, 16)], rem_r.at[pl.ds(i * 16, 16)], dsend.at[1], drecv.at[1], (to[i], t))
        cp.start()
    xb[REMOTE * SLOT : 1024, :] = sb[REMOTE * SLOT : 1024, :]
    rem_r[REMOTE * 16 : 512, :] = rem_s[REMOTE * 16 : 512, :]

    eye = ones_where(iota((512, 512), 0) == iota((512, 512), 1))

    def flip_tile(i, carry):
        part = pl.ds(pl.multiple_of(i * 256, 256), 256)
        sel[:, part] = mm_nt(eye, pw[part, :]).astype(BF)
        return carry

    lax.fori_loop(0, 4, flip_tile, 0)
    sel[:, 1024:1088] = mm_nt(eye, pw[1024:1088, :]).astype(BF)

    kb[...] = jnp.zeros_like(kb)
    for g in range(4):
        vb[:, g * 256 : g * 256 + 128] = jnp.zeros((1024, 128), BF)
        vb[:, g * 256 + 128 : g * 256 + 256] = jnp.ones((1024, 128), BF)
    first = flen[0]
    q_pos = iota((256, 1024), 0) + t * 256
    k_pos = iota((256, 1024), 1)
    q_late = jnp.where(q_pos >= first, 1, 0)
    k_late = jnp.where(k_pos >= first, 1, 0)
    bias[...] = jnp.where((q_late == k_late) & (k_pos <= q_pos), 0.0, -1e30)

    for d in (1, 2, 3):
        source_copies[d - 1].wait()
    eye256 = ones_where(iota((256, 256), 0) == iota((256, 256), 1))

    def pick_tile(b, carry):
        want = srcs[b] - e * 512
        oh[b] = mm_nt(eye256, ones_where(iota((512, 256), 0) == want)).astype(BF)
        return carry

    lax.fori_loop(0, 4, pick_tile, 0)

    remote(xb.at[pl.ds(0, REMOTE * SLOT)], xb.at[pl.ds(0, REMOTE * SLOT)], dsend.at[0], drecv.at[0], (to[0], t)).wait()
    remote(rem_r.at[pl.ds(0, REMOTE * 16)], rem_r.at[pl.ds(0, REMOTE * 16)], dsend.at[1], drecv.at[1], (to[0], t)).wait()
    down = {}
    for k in range(CHUNKS):
        cols = pl.ds(k * CW, CW)
        for d in (1, 3, 2):
            down[k, d] = remote(
                wd_hbm.at[side[d], :, cols], wd.at[d, :, cols], wsend.at[2 + k, d], wrecv.at[2 + k, d], (e, side[d])
            )
            down[k, d].start()
    row, col = iota((64, 512), 0), iota((64, 512), 1)
    same = ((col >> 4) == (row >> 1)) & ((row & 1) == (col & 1))
    for q in range(8):
        xb[1024:1088, q * 256 : (q + 1) * 256] = mm(
            ones_where(same & (((col >> 1) & 7) == q)), rem_r[...]
        ).astype(BF)

    for d in (0, 1, 3, 2):
        if d == 0:
            local[1].wait()
            local[2].wait()
        else:
            gate_up[0, d].wait()
            gate_up[1, d].wait()

        def hidden_tile(i, carry, d=d):
            rows = pl.ds(pl.multiple_of(i * 272, 16), 272)
            g = mm_nt(xb[rows, :], wg[d])
            u = mm_nt(xb[rows, :], wu[d])
            hb[d, rows, :] = (g / (1.0 + jnp.exp(-g)) * u).astype(BF)
            return carry

        lax.fori_loop(0, 4, hidden_tile, 0)

    local[3].wait()
    row, col = iota((256, 64), 0), iota((256, 64), 1)
    pack = [
        ones_where(((row >> 3) == (col >> 1)) & ((row & 1) == (col & 1)) & (((row >> 1) & 3) == q)) for q in range(4)
    ]
    row, col = iota((64, 256), 0), iota((64, 256), 1)
    unpack = [
        ones_where(((col >> 3) == (row >> 1)) & ((row & 1) == (col & 1)) & (((col >> 1) & 3) == q)) for q in range(4)
    ]
    for k in range(CHUNKS):
        cols = pl.ds(k * CW, CW)
        for d in (1, 3, 2):
            down[k, d].wait()

        def out_tile(i, carry, cols=cols):
            rows = pl.ds(pl.multiple_of(i * 272, 16), 272)
            o = mm(hb[0, rows, :], wd[0, :, cols])
            for d in (1, 3, 2):
                o = o + mm(hb[d, rows, :], wd[d, :, cols])
            sb[rows, cols] = o.astype(BF)
            return carry

        lax.fori_loop(0, 4, out_tile, 0)
        for i in range(REMOTE):
            cp = remote(
                sb.at[pl.ds(i * SLOT, SLOT), cols], rb.at[pl.ds(i * SLOT, SLOT), cols],
                rsend.at[0, k], rrecv.at[0, k], (back[i], t),
            )
            cp.start()
        last = sb[1024:1088, cols]
        packed = jnp.zeros((256, 128), F32)
        for q in range(4):
            packed = packed + mm(pack[q], last[:, q * 128 : (q + 1) * 128])
        orem[k] = packed
        for i in range(REMOTE):
            cp = remote(
                orem.at[k, pl.ds(i * 8, 8)], rrem.at[k, pl.ds(i * 8, 8)],
                rsend.at[1, k], rrecv.at[1, k], (back[i], t),
            )
            cp.start()
        rb[REMOTE * SLOT : 1024, cols] = sb[REMOTE * SLOT : 1024, cols]
        rrem[k, REMOTE * 8 : 256, :] = orem[k, REMOTE * 8 : 256, :]

    local[8].wait()
    for d in (1, 2, 3):

        @pl.when(t + d < 4)
        def _(d=d):
            remote(codec.at[t], codec.at[t], csend.at[d], crecv.at[d], (e, side[d])).start()

    local[4].wait()
    sums = {}
    own = pl.ds(pl.multiple_of(t * 128, 128), 128)
    hacc[...] = jnp.zeros_like(hacc)

    def finish_chunk(k):
        cols = pl.ds(k * CW, CW)
        total = ps[own, cols].astype(F32)
        for d in (1, 2, 3):
            sums[k, d].wait()
            total = total + pr[d, :, cols].astype(F32)
        done = total.astype(BF)
        thinker[:, cols] = done
        hacc[...] += mm(done, wh[cols, :])

    for k in range(CHUNKS):
        cols = pl.ds(k * CW, CW)
        remote(
            sb.at[pl.ds(0, REMOTE * SLOT), cols], rb.at[pl.ds(0, REMOTE * SLOT), cols],
            rsend.at[0, k], rrecv.at[0, k], (to[0], t),
        ).wait()
        remote(
            orem.at[k, pl.ds(0, REMOTE * 8)], rrem.at[k, pl.ds(0, REMOTE * 8)],
            rsend.at[1, k], rrecv.at[1, k], (to[0], t),
        ).wait()
        got = rrem[k].astype(BF)
        for q in range(4):
            rb[1024:1088, k * CW + q * 128 : k * CW + (q + 1) * 128] = mm(unpack[q], got).astype(BF)

        def sum_tile(i, carry, cols=cols):
            rows = pl.ds(pl.multiple_of(i * 128, 128), 128)
            ps[rows, cols] = mm(sel[rows, :], rb[:, cols]).astype(BF)
            return carry

        lax.fori_loop(0, 4, sum_tile, 0)
        for d in (1, 2, 3):
            rows = pl.ds(pl.multiple_of(side[d] * 128, 128), 128)
            sums[k, d] = remote(ps.at[rows, cols], pr.at[d, :, cols], psend.at[k, d], precv.at[k, d], (e, side[d]))
            sums[k, d].start()
        if k > 0:
            finish_chunk(k - 1)
    finish_chunk(CHUNKS - 1)
    ha[own, :] = hacc[...].astype(BF)
    handed = [remote(ha.at[own], ha.at[own], hsend.at[d], hrecv.at[d], (e, side[d])) for d in (1, 2, 3)]
    for cp in handed:
        cp.start()
    for d in (1, 2, 3):

        @pl.when(t + d < 4)
        def _(d=d):
            remote(codec.at[t], codec.at[t], csend.at[d], crecv.at[d], (e, side[d])).wait_send()

        @pl.when(t >= d)
        def _(d=d):
            remote(codec.at[t - d], codec.at[t - d], csend.at[d], crecv.at[d], (e, side[d])).wait_recv()

    for i in (5, 6, 7):
        local[i].wait()
    for cp in handed:
        cp.wait()

    def frame_tile(b, carry):
        rows = pl.ds(pl.multiple_of(b * 256, 256), 256)
        v = mm(oh[b], ha[...]) + codec[b].astype(F32)
        n = rms(v, tgain[...]).astype(BF)
        tn[rows, :] = n
        kv = mm(n, wkv[...])
        for g in range(4):
            kb[rows, g * 128 : (g + 1) * 128] = rms(kv[:, g * 128 : (g + 1) * 128], qkg[1:2, :]).astype(BF)
            vb[rows, g * 256 : g * 256 + 128] = kv[:, 512 + g * 128 : 640 + g * 128].astype(BF)
        return carry

    lax.fori_loop(0, t + 1, frame_tile, 0)
    mine = pl.ds(pl.multiple_of(t * 256, 256), 256)
    queries = mm(tn[mine, :], wq[...])
    for h in range(8):
        qb[:, h * 128 : (h + 1) * 128] = rms(queries[:, h * 128 : (h + 1) * 128], qkg[0:1, :]).astype(BF)

    def head(h, carry):
        lanes = pl.ds(pl.multiple_of(h * 128, 128), 128)
        keys = kb[:, pl.ds(pl.multiple_of((h >> 1) * 128, 128), 128)]
        s = mm_nt(qb[:, lanes], keys) * (128.0 ** -0.5) + bias[...]
        w = jnp.exp(s - jnp.max(s, axis=-1, keepdims=True)).astype(BF)
        o = mm(w, vb[:, pl.ds(pl.multiple_of((h >> 1) * 256, 256), 256)])
        at[:, lanes] = (o[:, :128] / o[:, 128:]).astype(BF)
        return carry

    lax.fori_loop(0, 8, head, 0)
    talker[...] = mm(at[...], wo[...]).astype(BF)


def per_device(
    tokens, norm_gain, expert_ids, route_weights, w_gate, w_up, w_down, codec_embeds,
    frame_lengths, source_rows, w_handover, talker_gain, w_query, w_kv, qk_gains, w_out,
):
    vm = pl.BlockSpec(memory_space=pltpu.VMEM)
    hb = pl.BlockSpec(memory_space=pl.ANY)
    sm = pl.BlockSpec(memory_space=pltpu.SMEM)
    dma = pltpu.SemaphoreType.DMA
    scratch = [
        ((512, 2048), BF),
        ((4, 192, 2048), BF),
        ((4, 192, 2048), BF),
        ((4, 192, 2048), BF),
        ((2048, 1024), BF),
        ((1024, 1024), BF),
        ((1024, 1024), BF),
        ((1024, 1024), BF),
        ((1088, 512), BF),
        ((512, 1088), BF),
        ((1088, 2048), BF),
        ((1088, 2048), BF),
        ((4, 1088, 192), BF),
        ((1088, 2048), BF),
        ((512, 256), BF),
        ((512, 256), BF),
        ((4, 256, 128), F32),
        ((4, 256, 128), F32),
        ((512, 2048), BF),
        ((4, 128, 2048), BF),
        ((128, 1024), F32),
        ((512, 1024), BF),
        ((4, 256, 1024), BF),
        ((4, 1, 256), jnp.int32),
        ((4, 256, 512), BF),
        ((1024, 1024), BF),
        ((1024, 512), BF),
        ((1024, 1024), BF),
        ((256, 1024), F32),
        ((256, 1024), BF),
        ((256, 1024), BF),
        ((8, 128), F32),
    ]
    sems = [(9,), (6, 4), (6, 4), (2,), (2,), (2, 4), (2, 4), (4, 4), (4, 4), (4,), (4,), (4,), (4,), (4,), (4,)]
    return pl.pallas_call(
        kernel,
        out_shape=(
            jax.ShapeDtypeStruct((128, 2048), BF),
            jax.ShapeDtypeStruct((256, 1024), BF),
        ),
        in_specs=[hb, vm, vm, vm, hb, hb, hb, hb, sm, vm, hb, vm, hb, hb, vm, hb],
        out_specs=(vm, vm),
        scratch_shapes=[pltpu.VMEM(s, d) for s, d in scratch] + [dma(s) for s in sems],
        compiler_params=pltpu.CompilerParams(
            collective_id=0, has_side_effects=True, vmem_limit_bytes=61 << 20
        ),
        cost_estimate=pl.CostEstimate(flops=20_000_000_000, bytes_accessed=40_000_000, transcendentals=4_000_000),
        name="expert_talker",
    )(
        tokens,
        norm_gain.reshape(1, 2048),
        expert_ids.T,
        route_weights.T,
        jnp.swapaxes(w_gate, 1, 2),
        jnp.swapaxes(w_up, 1, 2),
        w_down,
        codec_embeds,
        frame_lengths,
        source_rows.reshape(1, 256),
        w_handover,
        talker_gain.reshape(1, 1024),
        w_query,
        w_kv,
        qk_gains,
        w_out,
    )


def solution(mesh):
    placed = (
        P("expert", None),
        P(),
        P("expert", None),
        P("expert", None),
        P("expert", None, "tensor"),
        P("expert", None, "tensor"),
        P("expert", "tensor", None),
        P(("expert", "tensor"), None),
        P("expert"),
        P(("expert", "tensor")),
        P(),
        P(),
        P(),
        P(),
        P(),
        P(),
    )
    return jax.shard_map(
        per_device,
        mesh=mesh,
        in_specs=placed,
        out_specs=(P(("expert", "tensor"), None), P(("expert", "tensor"), None)),
        check_vma=False,
    )
```

```python
import math

import jax
import jax.numpy as jnp
from jax import lax
from jax.experimental import pallas as pl
from jax.experimental.pallas import tpu as pltpu
from jax.sharding import PartitionSpec as P

MESH = pl.DeviceIdType.MESH
BF = jnp.bfloat16
F32 = jnp.float32
EPS = 1e-06
GROUPS = 32
SLOT = 32
CHUNKS = 4
CW = 512
PIECES = ((0, 512, 0), (512, 512, 1), (1024, 512, 2), (1536, 256, 3), (1792, 256, None))
PAIRED = 3
STEP = (0, 1, 3, 2)


def peer_shifts():
    def opposite(s):
        return ((4 - s[0]) % 4, (4 - s[1]) % 4, s[2])

    every = [
        (dx, dz, dc)
        for dx in range(4)
        for dz in range(4)
        for dc in range(2)
        if (dx, dz, dc) != (0, 0, 0)
    ]
    order, seen = [], set()
    for s in sorted(every, key=lambda s: (sum(min(v, 4 - v) for v in s[:2]), s)):
        for one in (s, opposite(s)):
            if one not in seen:
                seen.add(one)
                order.append(one)
    return order[::-1]


SHIFTS = peer_shifts()
REMOTE = len(SHIFTS)


def mm(a, b):
    return jnp.dot(a, b, preferred_element_type=F32)


def mm_nt(a, b):
    return lax.dot_general(a, b, (((1,), (1,)), ((), ())), preferred_element_type=F32)


def iota(shape, dim):
    return lax.broadcasted_iota(jnp.int32, shape, dim)


def ones_where(cond):
    return jnp.where(cond, 1.0, 0.0).astype(BF)


def rms(v, gain):
    return v * lax.rsqrt(jnp.mean(v * v, axis=-1, keepdims=True) + EPS) * gain


def kernel(
    tok_hbm, gain, ids, rw, wg_hbm, wu_hbm, wd_hbm, codec_hbm, flen, src, wh_hbm, tgain, wq_hbm, wkv_hbm, qkg,
    thinker, at,
    tok, wg, wu, wd, wh, wq, wkv, pw, sel, sb, xb, hb, rb, rem_s, rem_r, orem, rrem, ps, pr,
    hacc, ha, codec, srcs, oh, tn, kb, vb, bias, qb,
    own_sem, wsend, wrecv, dsend, drecv, rsend, rrecv, psend, precv, qsend, qrecv, hsend, hrecv, csend, crecv, ssend, srecv,
):
    e = lax.axis_index("expert")
    t = lax.axis_index("tensor")
    x, z, c = e // 8, (e // 2) % 4, e % 2

    def shifted(s, sign):
        return (
            lax.rem(x + sign * s[0] + 4, 4) * 8
            + lax.rem(z + sign * s[1] + 4, 4) * 2
            + lax.rem(c + s[2], 2)
        )

    to = [shifted(s, 1) for s in SHIFTS]
    back = [shifted(s, -1) for s in SHIFTS]
    side = [t] + [lax.rem(t + d, 4) for d in (1, 2, 3)]

    barrier = pltpu.get_barrier_semaphore()
    for j in to:
        pl.semaphore_signal(barrier, inc=1, device_id=(j, t), device_id_type=MESH)
    for d in (1, 2, 3):
        pl.semaphore_signal(barrier, inc=1, device_id=(e, side[d]), device_id_type=MESH)

    local = [
        pltpu.make_async_copy(tok_hbm, tok, own_sem.at[0]),
        pltpu.make_async_copy(wg_hbm.at[t], wg.at[0], own_sem.at[1]),
        pltpu.make_async_copy(wu_hbm.at[t], wu.at[0], own_sem.at[2]),
        pltpu.make_async_copy(wd_hbm.at[t], wd.at[0], own_sem.at[3]),
        pltpu.make_async_copy(wh_hbm, wh, own_sem.at[4]),
        pltpu.make_async_copy(wkv_hbm, wkv, own_sem.at[5]),
        pltpu.make_async_copy(wq_hbm, wq, own_sem.at[6]),
        pltpu.make_async_copy(codec_hbm, codec.at[t], own_sem.at[7]),
    ]
    for cp in local:
        cp.start()

    def remote(a, b, s, r, device):
        return pltpu.make_async_remote_copy(
            src_ref=a, dst_ref=b, send_sem=s, recv_sem=r, device_id=device, device_id_type=MESH
        )

    slot_row = iota((GROUPS, 512), 0)
    wanted = jnp.full((GROUPS, 512), 4 * e + t, jnp.int32)
    for i in range(REMOTE):
        wanted = jnp.where(slot_row == i, 4 * to[i] + t, wanted)
    total = jnp.sum(rw[...], axis=0, keepdims=True)
    share = rw[...] / total
    chosen = jnp.zeros((GROUPS, 512), F32)
    weight = jnp.zeros((GROUPS, 512), F32)
    for k in range(8):
        hit = ids[k : k + 1, :] == wanted
        chosen = chosen + jnp.where(hit, 1.0, 0.0)
        weight = weight + jnp.where(hit, share[k : k + 1, :], 0.0)
    upper = ones_where(iota((512, 512), 0) < iota((512, 512), 1))
    rank = mm(chosen.astype(BF), upper)
    rank = jnp.where(chosen > 0.5, rank, -1.0).astype(BF)
    weight = weight.astype(BF)

    pl.semaphore_wait(barrier, REMOTE + 3)

    source_copies = [remote(src, srcs.at[t], ssend.at[d], srecv.at[d], (e, side[d])) for d in (1, 2, 3)]
    for cp in source_copies:
        cp.start()
    gate_up = {}
    for n in (1, 2, 3):
        d = STEP[n]
        for a, (h, v) in enumerate(((wg_hbm, wg), (wu_hbm, wu))):
            gate_up[a, n] = remote(h.at[side[d]], v.at[n], wsend.at[a, n], wrecv.at[a, n], (e, side[d]))
            gate_up[a, n].start()
    down = {}
    for k in range(CHUNKS):
        cols = pl.ds(k * CW, CW)
        for n in (1, 2, 3):
            d = STEP[n]
            down[k, n] = remote(
                wd_hbm.at[side[d], :, cols], wd.at[n, :, cols], wsend.at[2 + k, n], wrecv.at[2 + k, n], (e, side[d])
            )
            down[k, n].start()
    for d in (1, 2, 3):

        @pl.when(t + d < 4)
        def _(d=d):
            remote(codec_hbm, codec.at[t], csend.at[d], crecv.at[d], (e, side[d])).start()

    srcs[t] = src[...]

    local[0].wait()

    def norm_tile(i, carry):
        rows = pl.ds(pl.multiple_of(i * 64, 64), 64)
        tok[rows, :] = rms(tok[rows, :].astype(F32), gain[...]).astype(BF)
        return carry

    lax.fori_loop(0, 8, norm_tile, 0)

    def dispatch_tile(i, carry):
        rows = pl.ds(pl.multiple_of(i * 256, 256), 256)
        spread = ones_where(((iota((256, GROUPS), 0) + i * 256) >> 5) == iota((256, GROUPS), 1))
        place = (iota((256, 512), 0) & 31).astype(F32)
        hit = mm(spread, rank) == place
        pw[rows, :] = jnp.where(hit, mm(spread, weight), 0.0).astype(BF)
        sb[rows, :] = mm(ones_where(hit), tok[...]).astype(BF)
        return carry

    for g in range(4):
        dispatch_tile(g, 0)
        for i in range(8 * g, min(8 * g + 8, REMOTE)):
            cp = remote(
                sb.at[pl.ds(i * SLOT, SLOT)], xb.at[pl.ds(i * SLOT, SLOT)], dsend.at[0], drecv.at[g], (to[i], t)
            )
            cp.start()

    spread = ones_where((iota((64, GROUPS), 0) >> 1) == iota((64, GROUPS), 1))
    place = (iota((64, 512), 0) & 1).astype(F32) + 32.0
    hit = mm(spread, rank) == place
    pw[1024:1088, :] = jnp.where(hit, mm(spread, weight), 0.0).astype(BF)
    extra = mm(ones_where(hit), tok[...]).astype(BF)
    row, col = iota((512, 64), 0), iota((512, 64), 1)
    same = ((row >> 4) == (col >> 1)) & ((row & 1) == (col & 1))
    packed = jnp.zeros((512, 256), F32)
    for q in range(8):
        packed = packed + mm(ones_where(same & (((row >> 1) & 7) == q)), extra[:, q * 256 : (q + 1) * 256])
    rem_s[...] = packed.astype(BF)
    for i in range(REMOTE):
        cp = remote(rem_s.at[pl.ds(i * 16, 16)], rem_r.at[pl.ds(i * 16, 16)], dsend.at[1], drecv.at[4], (to[i], t))
        cp.start()
    xb[REMOTE * SLOT : 1024, :] = sb[REMOTE * SLOT : 1024, :]
    rem_r[REMOTE * 16 : 512, :] = rem_s[REMOTE * 16 : 512, :]

    eye = ones_where(iota((512, 512), 0) == iota((512, 512), 1))

    def flip_tile(i, carry):
        part = pl.ds(pl.multiple_of(i * 256, 256), 256)
        sel[:, part] = mm_nt(eye, pw[part, :]).astype(BF)
        return carry

    lax.fori_loop(0, 4, flip_tile, 0)
    sel[:, 1024:1088] = mm_nt(eye, pw[1024:1088, :]).astype(BF)

    kb[...] = jnp.zeros_like(kb)
    for g in range(4):
        vb[:, g * 256 : g * 256 + 128] = jnp.zeros((1024, 128), BF)
        vb[:, g * 256 + 128 : g * 256 + 256] = jnp.ones((1024, 128), BF)
    first = flen[0]
    q_pos = iota((256, 1024), 0) + t * 256
    k_pos = iota((256, 1024), 1)
    q_late = jnp.where(q_pos >= first, 1, 0)
    k_late = jnp.where(k_pos >= first, 1, 0)
    bias[...] = jnp.where((q_late == k_late) & (k_pos <= q_pos), 0.0, -1e30)

    for d in (1, 2, 3):
        source_copies[d - 1].wait()
    eye256 = ones_where(iota((256, 256), 0) == iota((256, 256), 1))

    def pick_tile(b, carry):
        want = srcs[b] - e * 512
        oh[b] = mm_nt(eye256, ones_where(iota((512, 256), 0) == want)).astype(BF)
        return carry

    lax.fori_loop(0, 4, pick_tile, 0)

    local[1].wait()
    local[2].wait()

    def hidden(n, rows):
        v = xb[rows, :]
        g = mm_nt(v, wg[n])
        u = mm_nt(v, wu[n])
        hb[n, rows, :] = (g / (1.0 + jnp.exp(-g)) * u).astype(BF)

    for n in (1, 2):
        gate_up[0, n].wait()
        gate_up[1, n].wait()
    for g in range(4):
        rows = pl.ds(g * 256, min(256, REMOTE * SLOT - g * 256))
        remote(xb.at[rows], xb.at[rows], dsend.at[0], drecv.at[g], (to[0], t)).wait_recv()

        def near(n, carry, g=g):
            hidden(n, pl.ds(g * 256, 256))
            return carry

        lax.fori_loop(0, 3, near, 0)
    remote(rem_r.at[pl.ds(0, REMOTE * 16)], rem_r.at[pl.ds(0, REMOTE * 16)], dsend.at[1], drecv.at[4], (to[0], t)).wait()
    row, col = iota((64, 512), 0), iota((64, 512), 1)
    same = ((col >> 4) == (row >> 1)) & ((row & 1) == (col & 1))
    for q in range(8):
        xb[1024:1088, q * 256 : (q + 1) * 256] = mm(
            ones_where(same & (((col >> 1) & 7) == q)), rem_r[...]
        ).astype(BF)

    def spare(n, carry):
        hidden(n, pl.ds(1024, 64))
        return carry

    lax.fori_loop(0, 3, spare, 0)
    gate_up[0, 3].wait()
    gate_up[1, 3].wait()

    def far(i, carry):
        hidden(3, pl.ds(pl.multiple_of(i * 272, 16), 272))
        return carry

    lax.fori_loop(0, 4, far, 0)
    remote(
        sb.at[pl.ds(0, REMOTE * SLOT)], xb.at[pl.ds(0, REMOTE * SLOT)], dsend.at[0], drecv.at[0], (to[0], t)
    ).wait_send()

    local[3].wait()
    row, col = iota((256, 64), 0), iota((256, 64), 1)
    pack = [
        ones_where(((row >> 3) == (col >> 1)) & ((row & 1) == (col & 1)) & (((row >> 1) & 3) == q)) for q in range(4)
    ]
    row, col = iota((64, 256), 0), iota((64, 256), 1)
    unpack = [
        ones_where(((col >> 3) == (row >> 1)) & ((row & 1) == (col & 1)) & (((col >> 1) & 3) == q)) for q in range(4)
    ]
    for k in range(CHUNKS):
        cols = pl.ds(k * CW, CW)
        for n in (1, 2, 3):
            down[k, n].wait()

        def out_tile(i, carry, cols=cols):
            rows = pl.ds(pl.multiple_of(i * 272, 16), 272)
            o = mm(hb[0, rows, :], wd[0, :, cols])
            for n in (1, 2, 3):
                o = o + mm(hb[n, rows, :], wd[n, :, cols])
            sb[rows, cols] = o.astype(BF)
            return carry

        lax.fori_loop(0, 4, out_tile, 0)
        last = sb[1024:1088, cols]
        packed = jnp.zeros((256, 128), F32)
        for q in range(4):
            packed = packed + mm(pack[q], last[:, q * 128 : (q + 1) * 128])
        orem[k] = packed
        for i in range(REMOTE):
            cp = remote(
                orem.at[k, pl.ds(i * 8, 8)], rrem.at[k, pl.ds(i * 8, 8)],
                rsend.at[1, k], rrecv.at[1, k], (back[i], t),
            )
            cp.start()
        for p, (begin, width, _) in enumerate(PIECES):
            if begin // CW == k:
                part = pl.ds(begin, width)
                for i in range(REMOTE):
                    cp = remote(
                        sb.at[pl.ds(i * SLOT, SLOT), part], rb.at[pl.ds(i * SLOT, SLOT), part],
                        rsend.at[0, p], rrecv.at[0, p], (back[i], t),
                    )
                    cp.start()
        rb[REMOTE * SLOT : 1024, cols] = sb[REMOTE * SLOT : 1024, cols]
        rrem[k, REMOTE * 8 : 256, :] = orem[k, REMOTE * 8 : 256, :]

    local[4].wait()
    sums = {}
    own = pl.ds(pl.multiple_of(t * 128, 128), 128)
    hacc[...] = jnp.zeros_like(hacc)

    pair = (t + 1 - 2 * (t % 2), 3 - t)
    cross = lax.rem(t + 2, 4)

    def block(who):
        return pl.ds(pl.multiple_of(who * 128, 128), 128)

    def halves(p):
        return [(h, pl.ds(PIECES[p][0] + h * 256, 256), pair[h], pair[1 - h]) for h in (0, 1)]

    def begin_sum(p):
        begin, width, _ = PIECES[p]
        if p < PAIRED:
            for h, cols, one, _ in halves(p):
                for n, who in ((1, cross), (0, one)):
                    sums[p, h, n] = remote(
                        ps.at[block(who), cols], pr.at[n, :, cols], psend.at[p, 2 * h + n], precv.at[p, 2 * h + n], (e, one)
                    )
                    sums[p, h, n].start()
            return
        cols = pl.ds(begin, width)
        for d in (2, 1, 3):
            sums[p, d] = remote(
                ps.at[block(side[d]), cols], pr.at[d, :, cols], psend.at[p, d], precv.at[p, d], (e, side[d])
            )
            sums[p, d].start()

    def middle(p):
        for h, cols, one, two in halves(p):
            sums[p, h, 1].wait()
            pr[2, :, cols] = (ps[block(two), cols].astype(F32) + pr[1, :, cols].astype(F32)).astype(BF)
            sums[p, h, 2] = remote(pr.at[2, :, cols], pr.at[3, :, cols], qsend.at[p, h], qrecv.at[p, h], (e, two))
            sums[p, h, 2].start()

    def finish(p):
        begin, width, _ = PIECES[p]
        cols = pl.ds(begin, width)
        if p < PAIRED:
            for h in (0, 1):
                sums[p, h, 0].wait()
                sums[p, h, 2].wait()
            total = ps[own, cols].astype(F32) + pr[0, :, cols].astype(F32) + pr[3, :, cols].astype(F32)
        else:
            total = ps[own, cols].astype(F32)
            for d in (1, 2, 3):
                sums[p, d].wait()
                total = total + pr[d, :, cols].astype(F32)
        done = total.astype(BF)
        thinker[:, cols] = done
        hacc[...] += mm(done, wh[cols, :])

    for p, (begin, width, k) in enumerate(PIECES):
        cols = pl.ds(begin, width)
        if k is not None:
            remote(
                orem.at[k, pl.ds(0, REMOTE * 8)], rrem.at[k, pl.ds(0, REMOTE * 8)],
                rsend.at[1, k], rrecv.at[1, k], (to[0], t),
            ).wait()
            got = rrem[k].astype(BF)
            for q in range(4):
                rb[1024:1088, k * CW + q * 128 : k * CW + (q + 1) * 128] = mm(unpack[q], got).astype(BF)
        remote(
            sb.at[pl.ds(0, REMOTE * SLOT), cols], rb.at[pl.ds(0, REMOTE * SLOT), cols],
            rsend.at[0, p], rrecv.at[0, p], (to[0], t),
        ).wait()

        def sum_tile(i, carry, cols=cols):
            rows = pl.ds(pl.multiple_of(i * 128, 128), 128)
            ps[rows, cols] = mm(sel[rows, :], rb[:, cols]).astype(BF)
            return carry

        lax.fori_loop(0, 4, sum_tile, 0)
        begin_sum(p)
        if 1 <= p <= PAIRED:
            middle(p - 1)
        if 2 <= p <= PAIRED:
            finish(p - 2)
        if p == PAIRED + 1:
            finish(p - 2)
            finish(p - 1)
    finish(len(PIECES) - 1)
    ha[own, :] = hacc[...].astype(BF)
    handed = [remote(ha.at[own], ha.at[own], hsend.at[d], hrecv.at[d], (e, side[d])) for d in (1, 2, 3)]
    for cp in handed:
        cp.start()
    for d in (1, 2, 3):

        @pl.when(t + d < 4)
        def _(d=d):
            remote(codec_hbm, codec.at[t], csend.at[d], crecv.at[d], (e, side[d])).wait_send()

        @pl.when(t >= d)
        def _(d=d):
            remote(codec_hbm, codec.at[t - d], csend.at[d], crecv.at[d], (e, side[d])).wait_recv()

    for i in (5, 6, 7):
        local[i].wait()
    for cp in handed:
        cp.wait()

    def frame_tile(b, carry):
        rows = pl.ds(pl.multiple_of(b * 256, 256), 256)
        v = mm(oh[b], ha[...]) + codec[b].astype(F32)
        n = rms(v, tgain[...]).astype(BF)
        tn[rows, :] = n
        kv = mm(n, wkv[...])
        for g in range(4):
            kb[rows, g * 128 : (g + 1) * 128] = rms(kv[:, g * 128 : (g + 1) * 128], qkg[1:2, :]).astype(BF)
            vb[rows, g * 256 : g * 256 + 128] = kv[:, 512 + g * 128 : 640 + g * 128].astype(BF)
        return carry

    lax.fori_loop(0, t + 1, frame_tile, 0)
    mine = pl.ds(pl.multiple_of(t * 256, 256), 256)
    queries = mm(tn[mine, :], wq[...])
    for h in range(8):
        scaled = rms(queries[:, h * 128 : (h + 1) * 128], qkg[0:1, :] * (128.0**-0.5 * math.log2(math.e)))
        qb[:, h * 128 : (h + 1) * 128] = scaled.astype(BF)

    for h in range(8):
        lanes = slice(h * 128, (h + 1) * 128)
        g = h // 2
        s = mm_nt(qb[:, lanes], kb[:, g * 128 : (g + 1) * 128]) + bias[...]
        w = jnp.exp2(s - jnp.max(s, axis=-1, keepdims=True)).astype(BF)
        o = mm(w, vb[:, g * 256 : (g + 1) * 256])
        at[:, lanes] = (o[:, :128] / o[:, 128:]).astype(BF)


def project(at, wo, thinker_in, thinker, talker):
    thinker[...] = thinker_in[...]
    talker[...] = mm(at[...], wo[...]).astype(BF)


def per_device(
    tokens, norm_gain, expert_ids, route_weights, w_gate, w_up, w_down, codec_embeds,
    frame_lengths, source_rows, w_handover, talker_gain, w_query, w_kv, qk_gains, w_out,
):
    vm = pl.BlockSpec(memory_space=pltpu.VMEM)
    hb = pl.BlockSpec(memory_space=pl.ANY)
    sm = pl.BlockSpec(memory_space=pltpu.SMEM)
    dma = pltpu.SemaphoreType.DMA
    scratch = [
        ((512, 2048), BF),
        ((4, 192, 2048), BF),
        ((4, 192, 2048), BF),
        ((4, 192, 2048), BF),
        ((2048, 1024), BF),
        ((1024, 1024), BF),
        ((1024, 1024), BF),
        ((1088, 512), BF),
        ((512, 1088), BF),
        ((1088, 2048), BF),
        ((1088, 2048), BF),
        ((4, 1088, 192), BF),
        ((1088, 2048), BF),
        ((512, 256), BF),
        ((512, 256), BF),
        ((4, 256, 128), F32),
        ((4, 256, 128), F32),
        ((512, 2048), BF),
        ((4, 128, 2048), BF),
        ((128, 1024), F32),
        ((512, 1024), BF),
        ((4, 256, 1024), BF),
        ((4, 1, 256), jnp.int32),
        ((4, 256, 512), BF),
        ((1024, 1024), BF),
        ((1024, 512), BF),
        ((1024, 1024), BF),
        ((256, 1024), F32),
        ((256, 1024), BF),
    ]
    sems = [(8,), (6, 4), (6, 4), (2,), (5,), (2, 5), (2, 5), (5, 4), (5, 4), (3, 2), (3, 2), (4,), (4,), (4,), (4,), (4,), (4,)]
    thinker, attended = pl.pallas_call(
        kernel,
        out_shape=(
            jax.ShapeDtypeStruct((128, 2048), BF),
            jax.ShapeDtypeStruct((256, 1024), BF),
        ),
        in_specs=[hb, vm, vm, vm, hb, hb, hb, hb, sm, vm, hb, vm, hb, hb, vm],
        out_specs=(vm, vm),
        scratch_shapes=[pltpu.VMEM(s, d) for s, d in scratch] + [dma(s) for s in sems],
        compiler_params=pltpu.CompilerParams(
            collective_id=0, has_side_effects=True, vmem_limit_bytes=61 << 20
        ),
        cost_estimate=pl.CostEstimate(flops=20_000_000_000, bytes_accessed=40_000_000, transcendentals=4_000_000),
        name="expert_talker",
    )(
        tokens,
        norm_gain.reshape(1, 2048),
        expert_ids.T,
        route_weights.T,
        jnp.swapaxes(w_gate, 1, 2),
        jnp.swapaxes(w_up, 1, 2),
        w_down,
        codec_embeds,
        frame_lengths,
        source_rows.reshape(1, 256),
        w_handover,
        talker_gain.reshape(1, 1024),
        w_query,
        w_kv,
        qk_gains,
    )
    return pl.pallas_call(
        project,
        out_shape=(
            jax.ShapeDtypeStruct((128, 2048), BF),
            jax.ShapeDtypeStruct((256, 1024), BF),
        ),
        in_specs=[vm, vm, vm],
        out_specs=(vm, vm),
        cost_estimate=pl.CostEstimate(flops=536_870_912, bytes_accessed=5_000_000, transcendentals=0),
        compiler_params=pltpu.CompilerParams(vmem_limit_bytes=61 << 20),
        name="project",
    )(attended, w_out, thinker)


def solution(mesh):
    placed = (
        P("expert", None),
        P(),
        P("expert", None),
        P("expert", None),
        P("expert", None, "tensor"),
        P("expert", None, "tensor"),
        P("expert", "tensor", None),
        P(("expert", "tensor"), None),
        P("expert"),
        P(("expert", "tensor")),
        P(),
        P(),
        P(),
        P(),
        P(),
        P(),
    )
    return jax.shard_map(
        per_device,
        mesh=mesh,
        in_specs=placed,
        out_specs=(P(("expert", "tensor"), None), P(("expert", "tensor"), None)),
        check_vma=False,
    )
```

```python
import math

import jax
import jax.numpy as jnp
from jax import lax
from jax.experimental import pallas as pl
from jax.experimental.pallas import tpu as pltpu
from jax.sharding import PartitionSpec as P

MESH = pl.DeviceIdType.MESH
BF = jnp.bfloat16
F32 = jnp.float32
EPS = 1e-06
GROUPS = 32
SLOT = 32
CHUNKS = 4
CW = 512
PIECES = ((0, 512, 0), (512, 512, None), (1024, 512, 1), (1536, 256, None), (1792, 256, None))
PAIRED = 3
STEP = (0, 1, 3, 2)


def peer_shifts():
    order = []
    for a, b in ((1, 2), (1, 1), (2, 2), (2, 0), (1, 0), (0, 0)):
        for _ in range(4):
            for c in (0, 1):
                if (a, b, c) != (0, 0, 0) and (a, b, c) not in order:
                    order.append((a, b, c))
            a, b = (4 - b) % 4, a
    return order


SHIFTS = peer_shifts()
REMOTE = len(SHIFTS)


def mm(a, b):
    return jnp.dot(a, b, preferred_element_type=F32)


def mm_nt(a, b):
    return lax.dot_general(a, b, (((1,), (1,)), ((), ())), preferred_element_type=F32)


def iota(shape, dim):
    return lax.broadcasted_iota(jnp.int32, shape, dim)


def ones_where(cond):
    return jnp.where(cond, 1.0, 0.0).astype(BF)


def rms(v, gain):
    return v * lax.rsqrt(jnp.mean(v * v, axis=-1, keepdims=True) + EPS) * gain


def kernel(
    tok_hbm, gain, ids, rw, wg_hbm, wu_hbm, wd_hbm, codec_hbm, flen, src, wh_hbm, tgain, wq_hbm, wkv_hbm, qkg,
    thinker, at,
    tok, wg, wu, wd, wh, wq, wkv, pw, sel, sb, xb, hb, rb, rem_s, rem_r, orem, rrem, ps, pr,
    hacc, ha, codec, srcs, oh, tn, kb, vb, bias, qb,
    own_sem, wsend, wrecv, dsend, drecv, rsend, rrecv, psend, precv, qsend, qrecv, hsend, hrecv, csend, crecv, ssend, srecv,
):
    e = lax.axis_index("expert")
    t = lax.axis_index("tensor")
    x, z, c = e // 8, (e // 2) % 4, e % 2

    def shifted(s, sign):
        return (
            lax.rem(x + sign * s[0] + 4, 4) * 8
            + lax.rem(z + sign * s[1] + 4, 4) * 2
            + lax.rem(c + s[2], 2)
        )

    to = [shifted(s, 1) for s in SHIFTS]
    back = [shifted(s, -1) for s in SHIFTS]
    side = [t] + [lax.rem(t + d, 4) for d in (1, 2, 3)]

    barrier = pltpu.get_barrier_semaphore()
    for j in to:
        pl.semaphore_signal(barrier, inc=1, device_id=(j, t), device_id_type=MESH)
    for d in (1, 2, 3):
        pl.semaphore_signal(barrier, inc=1, device_id=(e, side[d]), device_id_type=MESH)

    local = [
        pltpu.make_async_copy(tok_hbm, tok, own_sem.at[0]),
        pltpu.make_async_copy(wg_hbm.at[t], wg.at[0], own_sem.at[1]),
        pltpu.make_async_copy(wu_hbm.at[t], wu.at[0], own_sem.at[2]),
        pltpu.make_async_copy(wd_hbm.at[t], wd.at[0], own_sem.at[3]),
        pltpu.make_async_copy(wh_hbm, wh, own_sem.at[4]),
        pltpu.make_async_copy(wkv_hbm, wkv, own_sem.at[5]),
        pltpu.make_async_copy(wq_hbm, wq, own_sem.at[6]),
        pltpu.make_async_copy(codec_hbm, codec.at[t], own_sem.at[7]),
    ]
    for cp in local:
        cp.start()

    def remote(a, b, s, r, device):
        return pltpu.make_async_remote_copy(
            src_ref=a, dst_ref=b, send_sem=s, recv_sem=r, device_id=device, device_id_type=MESH
        )

    pl.semaphore_wait(barrier, REMOTE + 3)

    source_copies = [remote(src, srcs.at[t], ssend.at[d], srecv.at[d], (e, side[d])) for d in (1, 2, 3)]
    for cp in source_copies:
        cp.start()
    gate_up = {}
    for n in (1, 2, 3):
        d = STEP[n]
        for a, (h, v) in enumerate(((wg_hbm, wg), (wu_hbm, wu))):
            gate_up[a, n] = remote(h.at[side[d]], v.at[n], wsend.at[a, n], wrecv.at[a, n], (e, side[d]))
            gate_up[a, n].start()
    down = {}
    for k in range(CHUNKS):
        cols = pl.ds(k * CW, CW)
        for n in (1, 2, 3):
            d = STEP[n]
            down[k, n] = remote(
                wd_hbm.at[side[d], :, cols], wd.at[n, :, cols], wsend.at[2 + k, n], wrecv.at[2 + k, n], (e, side[d])
            )
            down[k, n].start()
    for d in (1, 2, 3):

        @pl.when(t + d < 4)
        def _(d=d):
            remote(codec_hbm, codec.at[t], csend.at[d], crecv.at[d], (e, side[d])).start()

    srcs[t] = src[...]

    slot_row = iota((GROUPS, 512), 0)
    wanted = jnp.full((GROUPS, 512), 4 * e + t, jnp.int32)
    for i in range(REMOTE):
        wanted = jnp.where(slot_row == i, 4 * to[i] + t, wanted)
    total = jnp.sum(rw[...], axis=0, keepdims=True)
    share = rw[...] / total
    chosen = jnp.zeros((GROUPS, 512), F32)
    weight = jnp.zeros((GROUPS, 512), F32)
    for k in range(8):
        hit = ids[k : k + 1, :] == wanted
        chosen = chosen + jnp.where(hit, 1.0, 0.0)
        weight = weight + jnp.where(hit, share[k : k + 1, :], 0.0)
    upper = ones_where(iota((512, 512), 0) < iota((512, 512), 1))
    rank = mm(chosen.astype(BF), upper)
    rank = jnp.where(chosen > 0.5, rank, -1.0).astype(BF)
    weight = weight.astype(BF)

    local[0].wait()

    def norm_tile(i, carry):
        rows = pl.ds(pl.multiple_of(i * 64, 64), 64)
        tok[rows, :] = rms(tok[rows, :].astype(F32), gain[...]).astype(BF)
        return carry

    lax.fori_loop(0, 8, norm_tile, 0)

    def dispatch_tile(i, carry):
        rows = pl.ds(pl.multiple_of(i * 256, 256), 256)
        spread = ones_where(((iota((256, GROUPS), 0) + i * 256) >> 5) == iota((256, GROUPS), 1))
        place = (iota((256, 512), 0) & 31).astype(F32)
        hit = mm(spread, rank) == place
        pw[rows, :] = jnp.where(hit, mm(spread, weight), 0.0).astype(BF)
        sb[rows, :] = mm(ones_where(hit), tok[...]).astype(BF)
        return carry

    for g in range(4):
        dispatch_tile(g, 0)
        for i, part in [
            (i, pl.ds(k * CW, CW)) for k in range(CHUNKS) for i in range(8 * g, min(8 * g + 8, REMOTE))
        ]:
            slot = pl.ds(i * SLOT, SLOT)
            remote(sb.at[slot, part], xb.at[slot, part], dsend.at[0], drecv.at[g], (to[i], t)).start()

    spread = ones_where((iota((64, GROUPS), 0) >> 1) == iota((64, GROUPS), 1))
    place = (iota((64, 512), 0) & 1).astype(F32) + 32.0
    hit = mm(spread, rank) == place
    pw[1024:1088, :] = jnp.where(hit, mm(spread, weight), 0.0).astype(BF)
    extra = mm(ones_where(hit), tok[...]).astype(BF)
    row, col = iota((512, 64), 0), iota((512, 64), 1)
    same = ((row >> 4) == (col >> 1)) & ((row & 1) == (col & 1))
    packed = jnp.zeros((512, 256), F32)
    for q in range(8):
        packed = packed + mm(ones_where(same & (((row >> 1) & 7) == q)), extra[:, q * 256 : (q + 1) * 256])
    rem_s[...] = packed.astype(BF)
    for i in range(REMOTE):
        cp = remote(rem_s.at[pl.ds(i * 16, 16)], rem_r.at[pl.ds(i * 16, 16)], dsend.at[1], drecv.at[4], (to[i], t))
        cp.start()
    xb[REMOTE * SLOT : 1024, :] = sb[REMOTE * SLOT : 1024, :]
    rem_r[REMOTE * 16 : 512, :] = rem_s[REMOTE * 16 : 512, :]

    eye = ones_where(iota((512, 512), 0) == iota((512, 512), 1))

    def flip_tile(i, carry):
        part = pl.ds(pl.multiple_of(i * 256, 256), 256)
        sel[:, part] = mm_nt(eye, pw[part, :]).astype(BF)
        return carry

    lax.fori_loop(0, 4, flip_tile, 0)
    sel[:, 1024:1088] = mm_nt(eye, pw[1024:1088, :]).astype(BF)

    kb[...] = jnp.zeros_like(kb)
    for g in range(4):
        vb[:, g * 256 : g * 256 + 128] = jnp.zeros((1024, 128), BF)
        vb[:, g * 256 + 128 : g * 256 + 256] = jnp.ones((1024, 128), BF)
    first = flen[0]
    q_pos = iota((256, 1024), 0) + t * 256
    k_pos = iota((256, 1024), 1)
    q_late = jnp.where(q_pos >= first, 1, 0)
    k_late = jnp.where(k_pos >= first, 1, 0)
    bias[...] = jnp.where((q_late == k_late) & (k_pos <= q_pos), 0.0, -1e30)

    for d in (1, 2, 3):
        source_copies[d - 1].wait()
    eye256 = ones_where(iota((256, 256), 0) == iota((256, 256), 1))

    def pick_tile(b, carry):
        want = srcs[b] - e * 512
        oh[b] = mm_nt(eye256, ones_where(iota((512, 256), 0) == want)).astype(BF)
        return carry

    lax.fori_loop(0, 4, pick_tile, 0)

    local[1].wait()
    local[2].wait()

    def hidden(n, rows):
        v = xb[rows, :]
        g = mm_nt(v, wg[n])
        u = mm_nt(v, wu[n])
        hb[n, rows, :] = (g / (1.0 + jnp.exp(-g)) * u).astype(BF)

    for n in (1, 2):
        gate_up[0, n].wait()
        gate_up[1, n].wait()
    for g in range(4):
        rows = pl.ds(g * 256, min(256, REMOTE * SLOT - g * 256))
        remote(xb.at[rows], xb.at[rows], dsend.at[0], drecv.at[g], (to[0], t)).wait_recv()

        def near(n, carry, g=g):
            hidden(n, pl.ds(g * 256, 256))
            return carry

        lax.fori_loop(0, 3, near, 0)
    remote(rem_r.at[pl.ds(0, REMOTE * 16)], rem_r.at[pl.ds(0, REMOTE * 16)], dsend.at[1], drecv.at[4], (to[0], t)).wait()
    row, col = iota((64, 512), 0), iota((64, 512), 1)
    same = ((col >> 4) == (row >> 1)) & ((row & 1) == (col & 1))
    for q in range(8):
        xb[1024:1088, q * 256 : (q + 1) * 256] = mm(
            ones_where(same & (((col >> 1) & 7) == q)), rem_r[...]
        ).astype(BF)

    def spare(n, carry):
        hidden(n, pl.ds(1024, 64))
        return carry

    lax.fori_loop(0, 3, spare, 0)
    gate_up[0, 3].wait()
    gate_up[1, 3].wait()

    def far(i, carry):
        hidden(3, pl.ds(pl.multiple_of(i * 272, 16), 272))
        return carry

    lax.fori_loop(0, 4, far, 0)
    remote(
        sb.at[pl.ds(0, REMOTE * SLOT)], xb.at[pl.ds(0, REMOTE * SLOT)], dsend.at[0], drecv.at[0], (to[0], t)
    ).wait_send()

    local[3].wait()
    row, col = iota((512, 64), 0), iota((512, 64), 1)
    pack_same = ((row >> 4) == (col >> 1)) & ((row & 1) == (col & 1))
    pack_q = (row >> 1) & 7
    row, col = iota((64, 512), 0), iota((64, 512), 1)
    unpack_same = ((col >> 4) == (row >> 1)) & ((row & 1) == (col & 1))
    unpack_q = (col >> 1) & 7
    for k in range(CHUNKS):
        cols = pl.ds(k * CW, CW)
        for n in (1, 2, 3):
            down[k, n].wait()

        def out_tile(i, carry, cols=cols):
            rows = pl.ds(pl.multiple_of(i * 272, 16), 272)
            o = mm(hb[0, rows, :], wd[0, :, cols])
            for n in (1, 2, 3):
                o = o + mm(hb[n, rows, :], wd[n, :, cols])
            sb[rows, cols] = o.astype(BF)
            return carry

        lax.fori_loop(0, 4, out_tile, 0)
        if k % 2 == 1:
            m = k // 2
            packed = jnp.zeros((512, 128), F32)
            for q in range(8):
                packed = packed + mm(
                    ones_where(pack_same & (pack_q == q)),
                    sb[1024:1088, m * 1024 + q * 128 : m * 1024 + (q + 1) * 128],
                )
            orem[m] = packed.astype(BF)
            for i in range(REMOTE):
                cp = remote(
                    orem.at[m, pl.ds(i * 16, 16)], rrem.at[m, pl.ds(i * 16, 16)],
                    rsend.at[1, m], rrecv.at[1, m], (back[i], t),
                )
                cp.start()
            rrem[m, REMOTE * 16 : 512, :] = orem[m, REMOTE * 16 : 512, :]
        for p, (begin, width, _) in enumerate(PIECES):
            if begin // CW == k:
                part = pl.ds(begin, width)
                for i in range(REMOTE):
                    cp = remote(
                        sb.at[pl.ds(i * SLOT, SLOT), part], rb.at[pl.ds(i * SLOT, SLOT), part],
                        rsend.at[0, p], rrecv.at[0, p], (back[i], t),
                    )
                    cp.start()
        rb[REMOTE * SLOT : 1024, cols] = sb[REMOTE * SLOT : 1024, cols]

    local[4].wait()
    sums = {}
    own = pl.ds(pl.multiple_of(t * 128, 128), 128)
    hacc[...] = jnp.zeros_like(hacc)

    pair = (t + 1 - 2 * (t % 2), 3 - t)
    cross = lax.rem(t + 2, 4)

    def block(who):
        return pl.ds(pl.multiple_of(who * 128, 128), 128)

    def halves(p):
        return [(h, pl.ds(PIECES[p][0] + h * 256, 256), pair[h], pair[1 - h]) for h in (0, 1)]

    def begin_sum(p):
        begin, width, _ = PIECES[p]
        if p < PAIRED:
            for h, cols, one, _ in halves(p):
                for n, who in ((1, cross), (0, one)):
                    sums[p, h, n] = remote(
                        ps.at[block(who), cols], pr.at[n, :, cols], psend.at[p, 2 * h + n], precv.at[p, 2 * h + n], (e, one)
                    )
                    sums[p, h, n].start()
            return
        cols = pl.ds(begin, width)
        for d in (2, 1, 3):
            sums[p, d] = remote(
                ps.at[block(side[d]), cols], pr.at[d, :, cols], psend.at[p, d], precv.at[p, d], (e, side[d])
            )
            sums[p, d].start()

    def middle(p):
        for h, cols, one, two in halves(p):
            sums[p, h, 1].wait()
            pr[2, :, cols] = (ps[block(two), cols].astype(F32) + pr[1, :, cols].astype(F32)).astype(BF)
            sums[p, h, 2] = remote(pr.at[2, :, cols], pr.at[3, :, cols], qsend.at[p, h], qrecv.at[p, h], (e, two))
            sums[p, h, 2].start()

    def finish(p):
        begin, width, _ = PIECES[p]
        cols = pl.ds(begin, width)
        if p < PAIRED:
            for h in (0, 1):
                sums[p, h, 0].wait()
                sums[p, h, 2].wait()
            total = ps[own, cols].astype(F32) + pr[0, :, cols].astype(F32) + pr[3, :, cols].astype(F32)
        else:
            total = ps[own, cols].astype(F32)
            for d in (1, 2, 3):
                sums[p, d].wait()
                total = total + pr[d, :, cols].astype(F32)
        done = total.astype(BF)
        thinker[:, cols] = done
        hacc[...] += mm(done, wh[cols, :])

    for p, (begin, width, m) in enumerate(PIECES):
        cols = pl.ds(begin, width)
        if m is not None:
            remote(
                orem.at[m, pl.ds(0, REMOTE * 16)], rrem.at[m, pl.ds(0, REMOTE * 16)],
                rsend.at[1, m], rrecv.at[1, m], (to[0], t),
            ).wait()
            for q in range(8):
                rb[1024:1088, m * 1024 + q * 128 : m * 1024 + (q + 1) * 128] = mm(
                    ones_where(unpack_same & (unpack_q == q)), rrem[m]
                ).astype(BF)
        remote(
            sb.at[pl.ds(0, REMOTE * SLOT), cols], rb.at[pl.ds(0, REMOTE * SLOT), cols],
            rsend.at[0, p], rrecv.at[0, p], (to[0], t),
        ).wait()

        def sum_tile(i, carry, cols=cols):
            rows = pl.ds(pl.multiple_of(i * 128, 128), 128)
            ps[rows, cols] = mm(sel[rows, :], rb[:, cols]).astype(BF)
            return carry

        lax.fori_loop(0, 4, sum_tile, 0)
        begin_sum(p)
        if 1 <= p <= PAIRED:
            middle(p - 1)
        if 2 <= p <= PAIRED:
            finish(p - 2)
        if p == PAIRED + 1:
            finish(p - 2)
            finish(p - 1)
    finish(len(PIECES) - 1)
    ha[own, :] = hacc[...].astype(BF)
    handed = [remote(ha.at[own], ha.at[own], hsend.at[d], hrecv.at[d], (e, side[d])) for d in (2, 1, 3)]
    for cp in handed:
        cp.start()
    for d in (1, 2, 3):

        @pl.when(t + d < 4)
        def _(d=d):
            remote(codec_hbm, codec.at[t], csend.at[d], crecv.at[d], (e, side[d])).wait_send()

        @pl.when(t >= d)
        def _(d=d):
            remote(codec_hbm, codec.at[t - d], csend.at[d], crecv.at[d], (e, side[d])).wait_recv()

    for i in (5, 6, 7):
        local[i].wait()
    for cp in handed:
        cp.wait()

    def frame_tile(b, carry):
        rows = pl.ds(pl.multiple_of(b * 256, 256), 256)
        v = mm(oh[b], ha[...]) + codec[b].astype(F32)
        n = rms(v, tgain[...]).astype(BF)
        tn[rows, :] = n
        kv = mm(n, wkv[...])
        for g in range(4):
            kb[rows, g * 128 : (g + 1) * 128] = rms(kv[:, g * 128 : (g + 1) * 128], qkg[1:2, :]).astype(BF)
            vb[rows, g * 256 : g * 256 + 128] = kv[:, 512 + g * 128 : 640 + g * 128].astype(BF)
        return carry

    lax.fori_loop(0, t + 1, frame_tile, 0)
    mine = pl.ds(pl.multiple_of(t * 256, 256), 256)
    queries = mm(tn[mine, :], wq[...])
    for h in range(8):
        scaled = rms(queries[:, h * 128 : (h + 1) * 128], qkg[0:1, :] * (128.0**-0.5 * math.log2(math.e)))
        qb[:, h * 128 : (h + 1) * 128] = scaled.astype(BF)

    for h in range(8):
        lanes = slice(h * 128, (h + 1) * 128)
        g = h // 2
        s = mm_nt(qb[:, lanes], kb[:, g * 128 : (g + 1) * 128]) + bias[...]
        w = jnp.exp2(s - jnp.max(s, axis=-1, keepdims=True)).astype(BF)
        o = mm(w, vb[:, g * 256 : (g + 1) * 256])
        at[:, lanes] = (o[:, :128] / o[:, 128:]).astype(BF)


def project(at_hbm, wo_hbm, thinker_hbm, thinker, talker, at, wo, sem):
    first = pltpu.make_async_copy(at_hbm, at, sem.at[0])
    second = pltpu.make_async_copy(thinker_hbm, thinker, sem.at[1])
    third = pltpu.make_async_copy(wo_hbm, wo, sem.at[2])
    first.start()
    third.start()
    second.start()
    first.wait()
    third.wait()
    talker[...] = mm(at[...], wo[...]).astype(BF)
    second.wait()


def per_device(
    tokens, norm_gain, expert_ids, route_weights, w_gate, w_up, w_down, codec_embeds,
    frame_lengths, source_rows, w_handover, talker_gain, w_query, w_kv, qk_gains, w_out,
):
    vm = pl.BlockSpec(memory_space=pltpu.VMEM)
    hb = pl.BlockSpec(memory_space=pl.ANY)
    sm = pl.BlockSpec(memory_space=pltpu.SMEM)
    dma = pltpu.SemaphoreType.DMA
    scratch = [
        ((512, 2048), BF),
        ((4, 192, 2048), BF),
        ((4, 192, 2048), BF),
        ((4, 192, 2048), BF),
        ((2048, 1024), BF),
        ((1024, 1024), BF),
        ((1024, 1024), BF),
        ((1088, 512), BF),
        ((512, 1088), BF),
        ((1088, 2048), BF),
        ((1088, 2048), BF),
        ((4, 1088, 192), BF),
        ((1088, 2048), BF),
        ((512, 256), BF),
        ((512, 256), BF),
        ((2, 512, 128), BF),
        ((2, 512, 128), BF),
        ((512, 2048), BF),
        ((4, 128, 2048), BF),
        ((128, 1024), F32),
        ((512, 1024), BF),
        ((4, 256, 1024), BF),
        ((4, 1, 256), jnp.int32),
        ((4, 256, 512), BF),
        ((1024, 1024), BF),
        ((1024, 512), BF),
        ((1024, 1024), BF),
        ((256, 1024), F32),
        ((256, 1024), BF),
    ]
    sems = [(8,), (6, 4), (6, 4), (2,), (5,), (2, 5), (2, 5), (5, 4), (5, 4), (3, 2), (3, 2), (4,), (4,), (4,), (4,), (4,), (4,)]
    thinker, attended = pl.pallas_call(
        kernel,
        out_shape=(
            jax.ShapeDtypeStruct((128, 2048), BF),
            jax.ShapeDtypeStruct((256, 1024), BF),
        ),
        in_specs=[hb, vm, vm, vm, hb, hb, hb, hb, sm, vm, hb, vm, hb, hb, vm],
        out_specs=(vm, vm),
        scratch_shapes=[pltpu.VMEM(s, d) for s, d in scratch] + [dma(s) for s in sems],
        compiler_params=pltpu.CompilerParams(
            collective_id=0, has_side_effects=True, vmem_limit_bytes=61 << 20
        ),
        cost_estimate=pl.CostEstimate(flops=20_000_000_000, bytes_accessed=40_000_000, transcendentals=4_000_000),
        name="expert_talker",
    )(
        tokens,
        norm_gain.reshape(1, 2048),
        expert_ids.T,
        route_weights.T,
        jnp.swapaxes(w_gate, 1, 2),
        jnp.swapaxes(w_up, 1, 2),
        w_down,
        codec_embeds,
        frame_lengths,
        source_rows.reshape(1, 256),
        w_handover,
        talker_gain.reshape(1, 1024),
        w_query,
        w_kv,
        qk_gains,
    )
    return pl.pallas_call(
        project,
        out_shape=(
            jax.ShapeDtypeStruct((128, 2048), BF),
            jax.ShapeDtypeStruct((256, 1024), BF),
        ),
        in_specs=[hb, hb, hb],
        out_specs=(vm, vm),
        scratch_shapes=[pltpu.VMEM((256, 1024), BF), pltpu.VMEM((1024, 1024), BF), dma((3,))],
        cost_estimate=pl.CostEstimate(flops=536_870_912, bytes_accessed=5_000_000, transcendentals=0),
        compiler_params=pltpu.CompilerParams(vmem_limit_bytes=61 << 20),
        name="project",
    )(attended, w_out, thinker)


def solution(mesh):
    placed = (
        P("expert", None),
        P(),
        P("expert", None),
        P("expert", None),
        P("expert", None, "tensor"),
        P("expert", None, "tensor"),
        P("expert", "tensor", None),
        P(("expert", "tensor"), None),
        P("expert"),
        P(("expert", "tensor")),
        P(),
        P(),
        P(),
        P(),
        P(),
        P(),
    )
    return jax.shard_map(
        per_device,
        mesh=mesh,
        in_specs=placed,
        out_specs=(P(("expert", "tensor"), None), P(("expert", "tensor"), None)),
        check_vma=False,
    )
```
